768 devices in a mesh: blk: 32 (over z_lo, x, core), narrow: 24 (over y, z_hi).
Axes of the slice: x: 4, y: 8, z: 12 (z_hi: 3, z_lo: 4; z = z_hi * 4 + z_lo), core: 2. Of those that a mesh axis runs over, the one named last changes fastest.
Arguments:
- image_features: bfloat16 [294912, 1152], P(('blk', 'narrow')), may hold values from -6 to 6
- head_weight: bfloat16 [1152, 1152], replicated, may hold values from -0.1875 to 0.1875
- text_embeddings: bfloat16 [294912, 1152], P(('blk', 'narrow')), may hold values from -0.1875 to 0.1875
- log_scale: float32 [1], replicated, may hold values from 1.5 to 2.5
- logit_bias: float32 [1], replicated, may hold values from -3 to -1
Outputs:
- text_grad: float32 [294912, 1152], P(('blk', 'narrow'))
- head_grad: float32 [1152, 1152], P('narrow', 'blk')
The draws below stay inside these ranges and needn't reach their ends.
All inputs are finite; a program needn't handle non-finite values.
Results may differ from the reference program's by a relative error of at most 0.0051.
Values may be sent and summed in bfloat16 or wider, within the bound.
A program may use at most 128 MiB of HBM per device.

```python
import jax
import jax.numpy as jnp
from jax import lax

D = 1152
F = 1152
ROWS = 384
BATCH = 294912
N_BLK = 32
N_NARROW = 24


def level_of(own_key, extent, cuts, smallest, largest):
    def one(axis_at, shards_of):
        heights = jax.random.uniform(jax.random.fold_in(jax.random.fold_in(own_key, 6), axis_at), (shards_of,), jnp.float32, smallest / len(cuts), largest / len(cuts))
        return jnp.repeat(jnp.exp(heights), extent[axis_at] // shards_of).reshape((-1,) + (1,) * (len(extent) - axis_at - 1))

    factor_of = one(*cuts[0])
    for cut in cuts[1:]:
        factor_of = factor_of * one(*cut)
    return factor_of


def gaussian(key, dims, width, limit, shards=(), kind=jnp.bfloat16):
    level = level_of(key, dims, shards, -0.22, 0.18) if shards else 1.0
    array = jax.random.normal(key, dims, jnp.float32) * width * level
    return jnp.minimum(jnp.maximum(array, -limit), limit).astype(kind)


def setup_inputs(seed: int = 0) -> dict:
    keys = jax.random.split(jax.random.key(seed), 6)
    return {
        "image_features": gaussian(keys[0], (BATCH, F), 1.0, 6.0, ((0, 768),)),
        "head_weight": gaussian(keys[1], (F, D), F ** -0.5, 0.1875),
        "text_embeddings": gaussian(keys[2], (BATCH, D), (D ** -0.5), 0.1875, ((0, 768),)),
        "log_scale": jnp.clip(jax.random.uniform(keys[3], (1,), jnp.float32, 1.5, 2.5), 1.5, 2.5),
        "logit_bias": jnp.clip(jax.random.uniform(keys[4], (1,), jnp.float32, -3.0, -1.0), -3.0, -1.0),
    }


norm_eps = 1e-06

def normalize(vector):
    inverse = lax.rsqrt(lax.optimization_barrier(jnp.sum(vector * vector, axis=-1, keepdims=True)) + norm_eps)
    return (vector * inverse, inverse)

def reference(image_features, head_weight, text_embeddings, log_scale, logit_bias):
    projected = jnp.dot(image_features, head_weight, preferred_element_type=jnp.float32)
    image_unit, image_inverse = normalize(projected)
    image_bf = image_unit.astype(jnp.bfloat16)
    text_unit, text_inverse = normalize(text_embeddings.astype(jnp.float32))
    text_bf = text_unit.astype(jnp.bfloat16)
    image_four = image_bf.reshape(N_BLK, N_NARROW, ROWS, D).astype(jnp.float32)
    text_four = text_bf.reshape(N_BLK, N_NARROW, ROWS, D).astype(jnp.float32)
    text_prev = jnp.roll(text_four, 1, axis=0)
    logit_scale = jnp.exp(log_scale[0])
    positives = 2.0 * jnp.eye(ROWS, dtype=jnp.float32) - 1.0
    negatives = -jnp.ones((ROWS, ROWS), jnp.float32)

    def pair_grads(text_block, labels):
        scores = logit_scale * jnp.einsum('bnid,bnjd->bnij', image_four, text_block) + logit_bias[0]
        coupling = (-labels * jax.nn.sigmoid(-labels * scores) * logit_scale).astype(jnp.bfloat16)
        coupling = coupling.astype(jnp.float32)
        image_part = jnp.einsum('bnij,bnjd->bnid', coupling, text_block)
        text_part = jnp.einsum('bnij,bnid->bnjd', coupling, image_four)
        return (image_part, text_part)
    image_first, text_first = pair_grads(text_four, positives)
    image_second, text_second = pair_grads(text_prev, negatives)
    image_total = (image_first + image_second).reshape(BATCH, D)
    text_total = (text_first + jnp.roll(text_second, -1, axis=0)).reshape(BATCH, D)
    text_grad = (text_total - text_unit * lax.optimization_barrier(jnp.sum(text_unit * text_total, axis=-1, keepdims=True))) * text_inverse
    image_delta = ((image_total - image_unit * lax.optimization_barrier(jnp.sum(image_unit * image_total, axis=-1, keepdims=True))) * image_inverse).astype(jnp.bfloat16)
    head_grad = jnp.dot(image_features.T, image_delta, preferred_element_type=jnp.float32)
    return (text_grad, head_grad)
```

```python
import jax
import jax.numpy as jnp
from jax import lax
from jax.experimental import pallas as pl
from jax.experimental.pallas import tpu as pltpu
from jax.sharding import PartitionSpec as P

MESH = pl.DeviceIdType.MESH
F32 = jnp.float32
BF = jnp.bfloat16
EPS = 1e-06
NX, NY, ZL, ZH = 4, 8, 4, 3
R = 384
D = 1152
CH = 384
NCH = D // CH
G = 36
PIECE = 128


def mm(a, b, dims):
    return lax.dot_general(a, b, (dims, ((), ())), preferred_element_type=F32)


NN = ((1,), (0,))
NT = ((1,), (1,))
TN = ((0,), (0,))


def kernel(
    x_hbm, w_hbm, t_hbm, ls_ref, lb_ref,
    tg_ref, hg_ref,
    xb, wb, traw, tb, proj, ib, cb, c1b, c2b, dyo, dys, dyr, dtf, pf, dtb, hacc,
    xs, xr, sc, zs, zf, zr, yf, ys, yr, hs, hr,
    lsem, x2s, x2r, fws, fwr, dts, dtr, pxs, pxr, pts, ptr, dyss, dyrs,
    xss, xrs, zss, zrs, yss, yrs, hss, hrs,
):
    blk = lax.axis_index("blk")
    nar = lax.axis_index("narrow")
    c = blk % 2
    x = (blk // 2) % NX
    zl = blk // (2 * NX)
    y = nar // ZH
    zh = nar % ZH

    def dev(x_, zl_, c_, y_, zh_):
        return ((zl_ * NX + x_) * 2 + c_, y_ * ZH + zh_)

    partner = dev(x, zl, 1 - c, y, zh)
    chip = blk // 2
    chips = NX * ZL
    prev = (chip + chips - 1) % chips
    nxt = (chip + 1) % chips

    bar = pltpu.get_barrier_semaphore()

    def hello(d):
        pl.semaphore_signal(bar, inc=1, device_id=d, device_id_type=MESH)

    lx = pltpu.make_async_copy(x_hbm, xb.at[pl.ds(pl.multiple_of(c * R, R), R)], lsem.at[0])
    lw = pltpu.make_async_copy(w_hbm, wb, lsem.at[1])
    lt = pltpu.make_async_copy(t_hbm, traw, lsem.at[2])
    lt.start()
    lx.start()
    lw.start()

    hello(partner)
    hello((nxt * 2, nar))
    for d in range(1, NX):
        hello(dev((x + d) % NX, zl, c, y, zh))
    for d in range(1, ZL):
        hello(dev(x, (zl + d) % ZL, c, y, zh))
    for d in range(1, NY):
        hello(dev(x, zl, c, (y + d) % NY, zh))
    for d in range(1, ZH):
        hello(dev(x, zl, c, y, (zh + d) % ZH))

    base = 1 + (NX - 1) + (ZL - 1) + (NY - 1) + (ZH - 1)

    @pl.when(c == 0)
    def _():
        pl.semaphore_wait(bar, base + 2)

    @pl.when(c == 1)
    def _():
        pl.semaphore_wait(bar, base)

    def rcopy(src, dst, ss, rs, device):
        return pltpu.make_async_remote_copy(
            src_ref=src, dst_ref=dst, send_sem=ss, recv_sem=rs, device_id=device, device_id_type=MESH
        )

    def x2copy(piece, core, slot):
        return rcopy(
            x_hbm.at[pl.ds(piece * PIECE, PIECE)],
            xb.at[pl.ds(2 * R + piece * PIECE, PIECE)],
            x2s.at[piece],
            x2r.at[slot],
            (prev * 2 + core, nar),
        )

    @pl.when(c == 0)
    def _():
        x2copy(0, 0, 0).start()
        x2copy(2, 1, 0).start()
        x2copy(1, 0, 1).start()

    own = pl.ds(pl.multiple_of(c * R, R), R)
    other = pl.ds(pl.multiple_of((1 - c) * R, R), R)
    px = rcopy(x_hbm, xb.at[own], pxs, pxr, partner)
    px.start()

    lt.wait()

    def text_unit():
        t = traw[...].astype(F32)
        inv = lax.rsqrt(jnp.sum(t * t, axis=-1, keepdims=True) + EPS)
        return t * inv, inv

    tb[own, :] = text_unit()[0].astype(BF)
    pt = rcopy(tb.at[own], tb.at[own], pts, ptr, partner)
    pt.start()

    scale = jnp.exp(jnp.full((1, R), ls_ref[0], F32))
    bias = lb_ref[0]

    def coupling(img, text, positive):
        s = scale * mm(img, text, NT) + bias
        if not positive:
            return (jax.nn.sigmoid(s) * scale).astype(BF)
        rows, cols = s.shape
        diag = lax.broadcasted_iota(jnp.int32, (rows, cols), 0) == lax.broadcasted_iota(
            jnp.int32, (rows, cols), 1
        )
        g = jax.nn.sigmoid(jnp.where(diag, -s, s))
        return (jnp.where(diag, -g, g) * scale).astype(BF)

    def project(rows, slot, n):
        a = xb[rows, :]
        total = jnp.zeros((n, 1), F32)
        for k in range(NCH):
            p = mm(a, wb[:, k * CH : (k + 1) * CH], NN)
            proj[slot, k * CH : (k + 1) * CH] = p
            total = total + jnp.sum(p * p, axis=-1, keepdims=True)
        inv = lax.rsqrt(total + EPS)
        ib[slot, :] = (proj[slot, :] * inv).astype(BF)
        return inv

    def delta_out(tot, slot, inv, col, n):
        unit = proj[slot, :] * inv
        dl = (tot - unit * jnp.sum(unit * tot, axis=-1, keepdims=True)) * inv
        dtf[:, 0:n] = dl.astype(BF).astype(F32).T
        for q in range(2):
            for xx in range(NX):
                for z in range(ZL):
                    o = ((z * NX + xx) * 2 + q) * G
                    pf[z * G : (z + 1) * G, 0:n] = dtf[o : o + G, 0:n]
                dtb[q, xx * ZL * G : (xx + 1) * ZL * G, col] = pf[:, 0:n].astype(BF)

    def dtcopy(col, i):
        return rcopy(
            dtb.at[1 - c, :, col], dtb.at[1 - c, :, col], dts.at[i], dtr.at[i], partner
        )

    lx.wait()
    lw.wait()
    first = pl.ds(0, R)
    inv0 = project(own, first, R)
    cb[...] = coupling(ib[first, :], tb[own, :], True)
    dyo[...] = mm(cb[...], tb[own, :], NN)
    pt.wait()

    @pl.when(c == 1)
    def _():
        c1b[...] = coupling(ib[first, :], tb[0:R, :], False)
        dyo[...] += mm(c1b[...], tb[0:R, :], NN)

    owncol = pl.ds(pl.multiple_of(c * R, R), R)
    delta_out(dyo[...], first, inv0, owncol, R)
    dt0 = dtcopy(owncol, 0)
    dt0.start()

    dyo[...] = mm(cb[...], ib[first, :], TN)

    @pl.when(c == 1)
    def _():
        dys[...] = mm(c1b[...], ib[first, :], TN).astype(BF)

    px.wait()
    dt0.wait()
    for k in range(NCH):
        ks = slice(k * CH, (k + 1) * CH)
        hacc[:, ks] = mm(dtb[c, :, 0 : 2 * R], xb[0 : 2 * R, ks], NN)

    def fwcopy(g, slot):
        rows = pl.ds(pl.multiple_of(2 * R + g * PIECE, PIECE), PIECE)
        return rcopy(xb.at[rows], xb.at[rows], fws.at[slot], fwr.at[slot], partner)

    def colof(g):
        return pl.ds(pl.multiple_of(2 * R + g * PIECE, PIECE), PIECE)

    def piece(g, slot):
        rcopy(
            x_hbm.at[pl.ds(0, PIECE)], xb.at[colof(g)], x2s.at[0], x2r.at[slot], partner
        ).wait_recv()
        fwcopy(g, slot).start()
        at = pl.ds(R + slot * PIECE, PIECE)
        inv = project(colof(g), at, PIECE)
        cp = coupling(ib[at, :], tb[R : 2 * R, :], False)
        c2b[slot * PIECE : (slot + 1) * PIECE, :] = cp
        delta_out(mm(cp, tb[R : 2 * R, :], NN), at, inv, colof(g), PIECE)
        dtcopy(colof(g), 1 + slot).start()

    piece(2 * c, 0)

    @pl.when(c == 0)
    def _():
        piece(1, 1)

    @pl.when(c == 0)
    def _():
        fwcopy(0, 0).wait_send()
        fwcopy(1, 1).wait_send()
        dtcopy(colof(0), 1).wait_send()
        dtcopy(colof(1), 2).wait_send()
        fwcopy(2, 0).wait_recv()
        dtcopy(colof(2), 1).wait_recv()

    @pl.when(c == 1)
    def _():
        fwcopy(2, 0).wait_send()
        dtcopy(colof(2), 1).wait_send()
        fwcopy(0, 0).wait_recv()
        fwcopy(1, 1).wait_recv()
        dtcopy(colof(0), 1).wait_recv()
        dtcopy(colof(1), 2).wait_recv()

    def xcopy(k, d):
        i = k * (NX - 1) + d - 1
        to = (x + d) % NX
        return rcopy(
            xs.at[k, to], xr.at[k, d - 1], xss.at[i], xrs.at[i], dev(to, zl, c, y, zh)
        )

    for k in range(NCH):
        ks = slice(k * CH, (k + 1) * CH)
        h = hacc[:, ks] + mm(dtb[c, :, 2 * R : 3 * R], xb[2 * R : 3 * R, ks], NN)
        hacc[:, ks] = h
        for xx in range(NX):
            xs[k, xx] = h[xx * ZL * G : (xx + 1) * ZL * G, :].astype(BF)
        for d in range(1, NX):
            xcopy(k, d).start()

    dyc = rcopy(dys, dyr, dyss, dyrs, partner)

    @pl.when(c == 0)
    def _():
        dys[...] = mm(c2b[...], ib[pl.ds(R, 2 * PIECE), :], TN).astype(BF)

    dyc.start()

    @pl.when(c == 1)
    def _():
        dyo[...] += mm(c2b[0:PIECE, :], ib[pl.ds(R, PIECE), :], TN)

    dyc.wait()
    tu, tinv = text_unit()
    tt = dyo[...] + dyr[...].astype(F32)
    tg_ref[...] = (tt - tu * jnp.sum(tu * tt, axis=-1, keepdims=True)) * tinv

    def zcopy(k, d):
        i = k * (ZL - 1) + d - 1
        to = (zl + d) % ZL
        return rcopy(
            zs.at[k, to], zr.at[k, d - 1], zss.at[i], zrs.at[i], dev(x, to, c, y, zh)
        )

    sc[ZL * G :, :] = jnp.zeros((16, CH), F32)
    rows = pl.ds(pl.multiple_of(x * ZL * G, ZL * G), ZL * G)
    for k in range(NCH):
        s = hacc[rows, k * CH : (k + 1) * CH]
        for d in range(1, NX):
            xcopy(k, d).wait_recv()
            s = s + xr[k, d - 1].astype(F32)
        sc[0 : ZL * G, :] = s
        for z in range(ZL):
            p = sc[z * G : z * G + 48, :]
            zf[k, z] = p
            zs[k, z] = p.astype(BF)
        for d in range(1, ZL):
            zcopy(k, d).start()

    for k in range(NCH):
        s = zf[k, zl]
        for d in range(1, ZL):
            zcopy(k, d).wait_recv()
            s = s + zr[k, d - 1].astype(F32)
        yf[:, k * CH : (k + 1) * CH] = s
        ys[:, k * CH : (k + 1) * CH] = s.astype(BF)

    def window(i):
        return pl.ds(pl.multiple_of(i * 128, 128), 256)

    def ycopy(d):
        to = (y + d) % NY
        return rcopy(
            ys.at[:, window(to)], yr.at[d - 1], yss.at[d - 1], yrs.at[d - 1], dev(x, zl, c, to, zh)
        )

    for d in range(1, NY):
        ycopy(d).start()
    s = yf[:, window(y)]
    for d in range(1, NY):
        ycopy(d).wait_recv()
        s = s + yr[d - 1].astype(F32)

    hs[...] = s.astype(BF)

    def hcopy(d):
        return rcopy(hs, hr.at[d - 1], hss.at[d - 1], hrs.at[d - 1], dev(x, zl, c, y, (zh + d) % ZH))

    for d in range(1, ZH):
        hcopy(d).start()
    for d in range(1, ZH):
        hcopy(d).wait_recv()
        s = s + hr[d - 1].astype(F32)
    s = pltpu.roll(s, (256 - (16 * y + 48 * zh)) % 256, 1)
    hg_ref[...] = s[:, 0:128].T[0:48, 0:G]

    @pl.when(c == 0)
    def _():
        for p, core, slot in ((0, 0, 0), (2, 1, 0), (1, 0, 1)):
            x2copy(p, core, slot).wait_send()

    for k in range(NCH):
        for d in range(1, NX):
            xcopy(k, d).wait_send()
        for d in range(1, ZL):
            zcopy(k, d).wait_send()
    for d in range(1, NY):
        ycopy(d).wait_send()
    for d in range(1, ZH):
        hcopy(d).wait_send()


def shards(image_features, head_weight, text_embeddings, log_scale, logit_bias):
    anyspec = pl.BlockSpec(memory_space=pl.ANY)
    smem = pl.BlockSpec(memory_space=pltpu.SMEM)
    vmem = pl.BlockSpec(memory_space=pltpu.VMEM)
    dma = pltpu.SemaphoreType.DMA
    V = pltpu.VMEM
    return pl.pallas_call(
        kernel,
        out_shape=(jax.ShapeDtypeStruct((R, D), F32), jax.ShapeDtypeStruct((48, G), F32)),
        in_specs=[anyspec, anyspec, anyspec, smem, smem],
        out_specs=(vmem, vmem),
        scratch_shapes=[
            V((3 * R, D), BF),
            V((D, D), BF),
            V((R, D), BF),
            V((2 * R, D), BF),
            V((R + 2 * PIECE, D), F32),
            V((R + 2 * PIECE, D), BF),
            V((R, R), BF),
            V((R, R), BF),
            V((2 * PIECE, R), BF),
            V((R, D), F32),
            V((R, D), BF),
            V((R, D), BF),
            V((D, R), F32),
            V((ZL * G, R), F32),
            V((2, D // 2, D), BF),
            V((D // 2, D), F32),
            V((NCH, NX, ZL * G, CH), BF),
            V((NCH, NX - 1, ZL * G, CH), BF),
            V((ZL * G + 16, CH), F32),
            V((NCH, ZL, 48, CH), BF),
            V((NCH, ZL, 48, CH), F32),
            V((NCH, ZL - 1, 48, CH), BF),
            V((48, D), F32),
            V((48, D), BF),
            V((NY - 1, 48, 256), BF),
            V((48, 256), BF),
            V((ZH - 1, 48, 256), BF),
            dma((3,)), dma((3,)), dma((2,)), dma((2,)), dma((2,)), dma((3,)), dma((3,)),
            dma, dma, dma, dma, dma, dma,
            dma((NCH * (NX - 1),)), dma((NCH * (NX - 1),)),
            dma((NCH * (ZL - 1),)), dma((NCH * (ZL - 1),)),
            dma((NY - 1,)), dma((NY - 1,)), dma((ZH - 1,)), dma((ZH - 1,)),
        ],
        compiler_params=pltpu.CompilerParams(
            collective_id=0, has_side_effects=True, vmem_limit_bytes=56 * 2**20
        ),
        name="siglip_backward",
    )(image_features, head_weight, text_embeddings, log_scale, logit_bias)


def solution(mesh):
    return jax.shard_map(
        shards,
        mesh=mesh,
        in_specs=(P(("blk", "narrow"), None), P(), P(("blk", "narrow"), None), P(), P()),
        out_specs=(P(("blk", "narrow"), None), P("narrow", "blk")),
        check_vma=False,
    )
```

```python
import jax
import jax.numpy as jnp
from jax import lax
from jax.experimental import pallas as pl
from jax.experimental.pallas import tpu as pltpu
from jax.sharding import PartitionSpec as P

MESH = pl.DeviceIdType.MESH
F32 = jnp.float32
BF = jnp.bfloat16
EPS = 1e-06
NX, NY, ZL, ZH = 4, 8, 4, 3
R = 384
D = 1152
CH = 384
NCH = D // CH
G = 36
PIECE = 128
CHUNKS = ((0, 512), (512, 384), (896, 256))
WINDOWS = ((0, 1, 2), (3, 4, 5), (6, 7))


def mm(a, b, dims):
    return lax.dot_general(a, b, (dims, ((), ())), preferred_element_type=F32)


NN = ((1,), (0,))
NT = ((1,), (1,))
TN = ((0,), (0,))


def kernel(
    x_hbm, w_hbm, t_hbm, ls_ref, lb_ref,
    tg_ref, hg_ref,
    xb, wb, traw, tb, proj, ib, cb, c1b, c2b, dyo, dys, dyr, dtf, pf, dtb, hacc,
    xs0, xs1, xs2, xr0, xr1, xr2, sc, zs0, zs1, zs2, zf, zr0, zr1, zr2, yf, ys, yr, hs, hf, hr,
    lsem, x2s, x2r, fws, fwr, dts, dtr, pxs, pxr, pts, ptr, dyss, dyrs,
    xss, xrs, zss, zrs, yss, yrs, hss, hrs,
):
    xs, xr, zs, zr = (xs0, xs1, xs2), (xr0, xr1, xr2), (zs0, zs1, zs2), (zr0, zr1, zr2)
    blk = lax.axis_index("blk")
    nar = lax.axis_index("narrow")
    c = blk % 2
    x = (blk // 2) % NX
    zl = blk // (2 * NX)
    y = nar // ZH
    zh = nar % ZH

    def dev(x_, zl_, c_, y_, zh_):
        return ((zl_ * NX + x_) * 2 + c_, y_ * ZH + zh_)

    partner = dev(x, zl, 1 - c, y, zh)
    chip = blk // 2
    chips = NX * ZL
    prev = (chip + chips - 1) % chips
    nxt = (chip + 1) % chips

    bar = pltpu.get_barrier_semaphore()

    def hello(d):
        pl.semaphore_signal(bar, inc=1, device_id=d, device_id_type=MESH)

    lx = pltpu.make_async_copy(x_hbm, xb.at[pl.ds(pl.multiple_of(c * R, R), R)], lsem.at[0])
    lw = pltpu.make_async_copy(w_hbm, wb, lsem.at[1])
    lt = pltpu.make_async_copy(t_hbm, traw, lsem.at[2])
    lt.start()
    lx.start()
    lw.start()

    hello(partner)
    hello((nxt * 2, nar))
    for d in range(1, NX):
        hello(dev((x + d) % NX, zl, c, y, zh))
    for d in range(1, ZL):
        hello(dev(x, (zl + d) % ZL, c, y, zh))
    for d in range(1, NY):
        hello(dev(x, zl, c, (y + d) % NY, zh))
    for d in range(1, ZH):
        hello(dev(x, zl, c, y, (zh + d) % ZH))

    base = 1 + (NX - 1) + (ZL - 1) + (NY - 1) + (ZH - 1)

    @pl.when(c == 0)
    def _():
        pl.semaphore_wait(bar, base + 2)

    @pl.when(c == 1)
    def _():
        pl.semaphore_wait(bar, base)

    def rcopy(src, dst, ss, rs, device):
        return pltpu.make_async_remote_copy(
            src_ref=src, dst_ref=dst, send_sem=ss, recv_sem=rs, device_id=device, device_id_type=MESH
        )

    def x2copy(piece, core, slot):
        return rcopy(
            x_hbm.at[pl.ds(piece * PIECE, PIECE)],
            xb.at[pl.ds(2 * R + piece * PIECE, PIECE)],
            x2s.at[piece],
            x2r.at[slot],
            (prev * 2 + core, nar),
        )

    @pl.when(c == 0)
    def _():
        x2copy(0, 0, 0).start()
        x2copy(2, 1, 0).start()
        x2copy(1, 0, 1).start()

    own = pl.ds(pl.multiple_of(c * R, R), R)
    other = pl.ds(pl.multiple_of((1 - c) * R, R), R)
    px = rcopy(x_hbm, xb.at[own], pxs, pxr, partner)
    px.start()

    lt.wait()

    def text_unit():
        t = traw[...].astype(F32)
        inv = lax.rsqrt(jnp.sum(t * t, axis=-1, keepdims=True) + EPS)
        return t * inv, inv

    tb[own, :] = text_unit()[0].astype(BF)
    pt = rcopy(tb.at[own], tb.at[own], pts, ptr, partner)
    pt.start()

    scale = jnp.exp(jnp.full((1, R), ls_ref[0], F32))
    bias = lb_ref[0]

    def coupling(img, text, positive):
        s = scale * mm(img, text, NT) + bias
        if not positive:
            return (jax.nn.sigmoid(s) * scale).astype(BF)
        rows, cols = s.shape
        diag = lax.broadcasted_iota(jnp.int32, (rows, cols), 0) == lax.broadcasted_iota(
            jnp.int32, (rows, cols), 1
        )
        g = jax.nn.sigmoid(jnp.where(diag, -s, s))
        return (jnp.where(diag, -g, g) * scale).astype(BF)

    def project(rows, slot, n):
        a = xb[rows, :]
        total = jnp.zeros((n, 1), F32)
        for k in range(NCH):
            p = mm(a, wb[:, k * CH : (k + 1) * CH], NN)
            proj[slot, k * CH : (k + 1) * CH] = p
            total = total + jnp.sum(p * p, axis=-1, keepdims=True)
        inv = lax.rsqrt(total + EPS)
        ib[slot, :] = (proj[slot, :] * inv).astype(BF)
        return inv

    def delta_out(tot, slot, inv, col, n):
        unit = proj[slot, :] * inv
        dl = (tot - unit * jnp.sum(unit * tot, axis=-1, keepdims=True)) * inv
        dtf[:, 0:n] = dl.astype(BF).astype(F32).T
        for q in range(2):
            for xx in range(NX):
                for z in range(ZL):
                    o = ((z * NX + xx) * 2 + q) * G
                    pf[z * G : (z + 1) * G, 0:n] = dtf[o : o + G, 0:n]
                dtb[q, xx * ZL * G : (xx + 1) * ZL * G, col] = pf[:, 0:n].astype(BF)

    def dtcopy(col, i):
        return rcopy(
            dtb.at[1 - c, :, col], dtb.at[1 - c, :, col], dts.at[i], dtr.at[i], partner
        )

    lx.wait()
    lw.wait()
    first = pl.ds(0, R)
    inv0 = project(own, first, R)
    cb[...] = coupling(ib[first, :], tb[own, :], True)
    dyo[...] = mm(cb[...], tb[own, :], NN)
    pt.wait()

    @pl.when(c == 1)
    def _():
        c1b[...] = coupling(ib[first, :], tb[0:R, :], False)
        dyo[...] += mm(c1b[...], tb[0:R, :], NN)

    owncol = pl.ds(pl.multiple_of(c * R, R), R)
    delta_out(dyo[...], first, inv0, owncol, R)
    dt0 = dtcopy(owncol, 0)
    dt0.start()

    dyo[...] = mm(cb[...], ib[first, :], TN)

    @pl.when(c == 1)
    def _():
        dys[...] = mm(c1b[...], ib[first, :], TN).astype(BF)

    px.wait()
    dt0.wait()
    for k in range(NCH):
        ks = slice(k * CH, (k + 1) * CH)
        hacc[:, ks] = mm(dtb[c, :, 0 : 2 * R], xb[0 : 2 * R, ks], NN)

    def fwcopy(g, slot):
        rows = pl.ds(pl.multiple_of(2 * R + g * PIECE, PIECE), PIECE)
        return rcopy(xb.at[rows], xb.at[rows], fws.at[slot], fwr.at[slot], partner)

    def colof(g):
        return pl.ds(pl.multiple_of(2 * R + g * PIECE, PIECE), PIECE)

    def piece(g, slot):
        rcopy(
            x_hbm.at[pl.ds(0, PIECE)], xb.at[colof(g)], x2s.at[0], x2r.at[slot], partner
        ).wait_recv()
        fwcopy(g, slot).start()
        at = pl.ds(R + slot * PIECE, PIECE)
        inv = project(colof(g), at, PIECE)
        cp = coupling(ib[at, :], tb[R : 2 * R, :], False)
        c2b[slot * PIECE : (slot + 1) * PIECE, :] = cp
        delta_out(mm(cp, tb[R : 2 * R, :], NN), at, inv, colof(g), PIECE)
        dtcopy(colof(g), 1 + slot).start()

    piece(2 * c, 0)

    @pl.when(c == 0)
    def _():
        piece(1, 1)

    @pl.when(c == 0)
    def _():
        fwcopy(0, 0).wait_send()
        fwcopy(1, 1).wait_send()
        dtcopy(colof(0), 1).wait_send()
        dtcopy(colof(1), 2).wait_send()
        fwcopy(2, 0).wait_recv()
        dtcopy(colof(2), 1).wait_recv()

    @pl.when(c == 1)
    def _():
        fwcopy(2, 0).wait_send()
        dtcopy(colof(2), 1).wait_send()
        fwcopy(0, 0).wait_recv()
        fwcopy(1, 1).wait_recv()
        dtcopy(colof(0), 1).wait_recv()
        dtcopy(colof(1), 2).wait_recv()

    def xcopy(k, d):
        i = k * (NX - 1) + d - 1
        to = (x + d) % NX
        return rcopy(
            xs[k].at[to], xr[k].at[d - 1], xss.at[i], xrs.at[i], dev(to, zl, c, y, zh)
        )

    for k, (o, w) in enumerate(CHUNKS):
        ks = slice(o, o + w)
        h = hacc[:, ks] + mm(dtb[c, :, 2 * R : 3 * R], xb[2 * R : 3 * R, ks], NN)
        hacc[:, ks] = h
        for xx in range(NX):
            xs[k][xx] = h[xx * ZL * G : (xx + 1) * ZL * G, :].astype(BF)
        for d in (2, 1, 3):
            xcopy(k, d).start()

    dyc = rcopy(dys, dyr, dyss, dyrs, partner)

    @pl.when(c == 0)
    def _():
        dys[...] = mm(c2b[...], ib[pl.ds(R, 2 * PIECE), :], TN).astype(BF)

    dyc.start()

    @pl.when(c == 1)
    def _():
        dyo[...] += mm(c2b[0:PIECE, :], ib[pl.ds(R, PIECE), :], TN)

    dyc.wait()
    tu, tinv = text_unit()
    tt = dyo[...] + dyr[...].astype(F32)
    tg_ref[...] = (tt - tu * jnp.sum(tu * tt, axis=-1, keepdims=True)) * tinv

    def zcopy(k, d):
        i = k * (ZL - 1) + d - 1
        to = (zl + d) % ZL
        return rcopy(
            zs[k].at[to], zr[k].at[d - 1], zss.at[i], zrs.at[i], dev(x, to, c, y, zh)
        )

    def ycopy(to):
        slot = (y - to + NY) % NY - 1
        return rcopy(
            ys.at[:, to * 128 : to * 128 + 256],
            yr.at[slot],
            yss.at[to],
            yrs.at[slot],
            dev(x, zl, c, to, zh),
        )

    sc[ZL * G :, :] = jnp.zeros((16, sc.shape[1]), F32)
    rows = pl.ds(pl.multiple_of(x * ZL * G, ZL * G), ZL * G)

    def after_x(k):
        o, w = CHUNKS[k]
        s = hacc[rows, o : o + w]
        for d in range(1, NX):
            xcopy(k, d).wait_recv()
            s = s + xr[k][d - 1].astype(F32)
        sc[0 : ZL * G, 0:w] = s
        for z in range(ZL):
            p = sc[z * G : z * G + 48, 0:w]
            zf[z, :, o : o + w] = p
            zs[k][z] = p.astype(BF)
        for d in range(1, ZL):
            zcopy(k, d).start()

    def after_z(k):
        o, w = CHUNKS[k]
        s = zf[zl, :, o : o + w]
        for d in range(1, ZL):
            zcopy(k, d).wait_recv()
            s = s + zr[k][d - 1].astype(F32)
        yf[:, o : o + w] = s
        ys[:, o : o + w] = s.astype(BF)
        for to in WINDOWS[k]:
            pl.when(y != to)(ycopy(to).start)

    after_x(0)
    after_x(1)
    after_z(0)
    after_x(2)
    after_z(1)
    after_z(2)
    s = yf[:, pl.ds(pl.multiple_of(y * 128, 128), 256)]
    for d in range(1, NY):
        rcopy(ys.at[:, 0:256], yr.at[d - 1], yss.at[0], yrs.at[d - 1], partner).wait_recv()
        s = s + yr[d - 1].astype(F32)

    for z in range(ZH):
        p = pltpu.roll(s, (256 - (16 * y + 48 * z)) % 256, 1)[:, 0:128]
        hf[z] = p
        hs[z] = p.astype(BF)

    def hcopy(d):
        to = (zh + d) % ZH
        return rcopy(hs.at[to], hr.at[d - 1], hss.at[d - 1], hrs.at[d - 1], dev(x, zl, c, y, to))

    for d in range(1, ZH):
        hcopy(d).start()
    s = hf[zh]
    for d in range(1, ZH):
        hcopy(d).wait_recv()
        s = s + hr[d - 1].astype(F32)
    hg_ref[...] = s[0:G, 0:48]

    @pl.when(c == 0)
    def _():
        for p, core, slot in ((0, 0, 0), (2, 1, 0), (1, 0, 1)):
            x2copy(p, core, slot).wait_send()

    for k in range(NCH):
        for d in range(1, NX):
            xcopy(k, d).wait_send()
        for d in range(1, ZL):
            zcopy(k, d).wait_send()
    for to in range(NY):
        pl.when(y != to)(ycopy(to).wait_send)
    for d in range(1, ZH):
        hcopy(d).wait_send()


def shards(image_features, head_weight, text_embeddings, log_scale, logit_bias):
    hbm = pl.BlockSpec(memory_space=pltpu.HBM)
    vmem = pl.BlockSpec(memory_space=pltpu.VMEM)
    smem = pl.BlockSpec(memory_space=pltpu.SMEM)
    dma = pltpu.SemaphoreType.DMA
    V = pltpu.VMEM
    text_grad, head_t = pl.pallas_call(
        kernel,
        out_shape=(pltpu.VMEM((R, D), F32), pltpu.VMEM((G, 48), F32)),
        in_specs=[hbm, hbm, hbm, smem, smem],
        out_specs=(vmem, vmem),
        scratch_shapes=[
            V((3 * R, D), BF),
            V((D, D), BF),
            V((R, D), BF),
            V((2 * R, D), BF),
            V((R + 2 * PIECE, D), F32),
            V((R + 2 * PIECE, D), BF),
            V((R, R), BF),
            V((R, R), BF),
            V((2 * PIECE, R), BF),
            V((R, D), F32),
            V((R, D), BF),
            V((R, D), BF),
            V((D, R), F32),
            V((ZL * G, R), F32),
            V((2, D // 2, D), BF),
            V((D // 2, D), F32),
            *[V((NX, ZL * G, w), BF) for _, w in CHUNKS],
            *[V((NX - 1, ZL * G, w), BF) for _, w in CHUNKS],
            V((ZL * G + 16, max(w for _, w in CHUNKS)), F32),
            *[V((ZL, 48, w), BF) for _, w in CHUNKS],
            V((ZL, 48, D), F32),
            *[V((ZL - 1, 48, w), BF) for _, w in CHUNKS],
            V((48, D), F32),
            V((48, D), BF),
            V((NY - 1, 48, 256), BF),
            V((ZH, 48, 128), BF),
            V((ZH, 48, 128), F32),
            V((ZH - 1, 48, 128), BF),
            dma((3,)), dma((3,)), dma((2,)), dma((2,)), dma((2,)), dma((3,)), dma((3,)),
            dma, dma, dma, dma, dma, dma,
            dma((NCH * (NX - 1),)), dma((NCH * (NX - 1),)),
            dma((NCH * (ZL - 1),)), dma((NCH * (ZL - 1),)),
            dma((NY,)), dma((NY - 1,)), dma((ZH - 1,)), dma((ZH - 1,)),
        ],
        compiler_params=pltpu.CompilerParams(
            collective_id=0, has_side_effects=True, vmem_limit_bytes=44 * 2**20
        ),
        name="siglip_backward",
    )(
        *(
            pltpu.with_memory_space_constraint(a, pltpu.HBM)
            for a in (image_features, head_weight, text_embeddings)
        ),
        log_scale,
        logit_bias,
    )
    return text_grad, head_t.T


def solution(mesh):
    return jax.shard_map(
        shards,
        mesh=mesh,
        in_specs=(P(("blk", "narrow"), None), P(), P(("blk", "narrow"), None), P(), P()),
        out_specs=(P(("blk", "narrow"), None), P("narrow", "blk")),
        check_vma=False,
    )
```

```python
import jax
import jax.numpy as jnp
from jax import lax
from jax.experimental import pallas as pl
from jax.experimental.pallas import tpu as pltpu
from jax.sharding import PartitionSpec as P

MESH = pl.DeviceIdType.MESH
F32 = jnp.float32
BF = jnp.bfloat16
EPS = 1e-06
NX, NY, ZL, ZH = 4, 8, 4, 3
R = 384
D = 1152
CH = 384
NCH = D // CH
G = 36
PIECE = 128
CHUNKS = ((0, 384), (384, 384))
WINDOWS = ((0, 1), (2, 3, 4))
FIRST, WIDE = D - 384, 384
LAST_WINDOWS = (5, 6, 7)


def mm(a, b, dims):
    return lax.dot_general(a, b, (dims, ((), ())), preferred_element_type=F32)


NN = ((1,), (0,))
NT = ((1,), (1,))
TN = ((0,), (0,))


def kernel(
    x_hbm, w_hbm, t_hbm, ls_ref, lb_ref,
    tg_ref, hg_ref,
    xb, wb, traw, tb, proj, ib, cb, c1b, c2b, dyo, dys, dyr, dtf, pf, dtb, hacc,
    xs0, xs1, xr0, xr1, sc, zs0, zs1, zf, zr0, zr1, yf, ys, yr, hs, hf, hr,
    za, zaf, zar, xa, xaf, xar,
    lsem, x2s, x2r, fws, fwr, dts, dtr, pxs, pxr, pts, ptr, dyss, dyrs,
    zas, zars, xas, xars, xss, xrs, zss, zrs, yss, yrs, hss, hrs,
):
    xs, xr, zs, zr = (xs0, xs1), (xr0, xr1), (zs0, zs1), (zr0, zr1)
    blk = lax.axis_index("blk")
    nar = lax.axis_index("narrow")
    c = blk % 2
    x = (blk // 2) % NX
    zl = blk // (2 * NX)
    y = nar // ZH
    zh = nar % ZH

    def dev(x_, zl_, c_, y_, zh_):
        return ((zl_ * NX + x_) * 2 + c_, y_ * ZH + zh_)

    partner = dev(x, zl, 1 - c, y, zh)
    chip = blk // 2
    chips = NX * ZL
    prev = (chip + chips - 1) % chips
    nxt = (chip + 1) % chips

    bar = pltpu.get_barrier_semaphore()

    def hello(d):
        pl.semaphore_signal(bar, inc=1, device_id=d, device_id_type=MESH)

    lx = pltpu.make_async_copy(x_hbm, xb.at[pl.ds(pl.multiple_of(c * R, R), R)], lsem.at[0])
    lw = pltpu.make_async_copy(w_hbm, wb, lsem.at[1])
    lt = pltpu.make_async_copy(t_hbm, traw, lsem.at[2])
    lt.start()
    lx.start()
    lw.start()

    hello(partner)
    hello((nxt * 2, nar))
    for d in range(1, NX):
        hello(dev((x + d) % NX, zl, c, y, zh))
    for d in range(1, ZL):
        hello(dev(x, (zl + d) % ZL, c, y, zh))
    for d in range(1, NY):
        hello(dev(x, zl, c, (y + d) % NY, zh))
    for d in range(1, ZH):
        hello(dev(x, zl, c, y, (zh + d) % ZH))

    base = 1 + (NX - 1) + (ZL - 1) + (NY - 1) + (ZH - 1)

    @pl.when(c == 0)
    def _():
        pl.semaphore_wait(bar, base + 2)

    @pl.when(c == 1)
    def _():
        pl.semaphore_wait(bar, base)

    def rcopy(src, dst, ss, rs, device):
        return pltpu.make_async_remote_copy(
            src_ref=src, dst_ref=dst, send_sem=ss, recv_sem=rs, device_id=device, device_id_type=MESH
        )

    def x2copy(piece, core, slot):
        return rcopy(
            x_hbm.at[pl.ds(piece * PIECE, PIECE)],
            xb.at[pl.ds(2 * R + piece * PIECE, PIECE)],
            x2s.at[piece],
            x2r.at[slot],
            (prev * 2 + core, nar),
        )

    @pl.when(c == 0)
    def _():
        x2copy(0, 0, 0).start()
        x2copy(2, 1, 0).start()
        x2copy(1, 0, 1).start()

    own = pl.ds(pl.multiple_of(c * R, R), R)
    other = pl.ds(pl.multiple_of((1 - c) * R, R), R)
    px = rcopy(x_hbm, xb.at[own], pxs, pxr, partner)
    px.start()

    lt.wait()

    def text_unit():
        t = traw[...].astype(F32)
        inv = lax.rsqrt(jnp.sum(t * t, axis=-1, keepdims=True) + EPS)
        return t * inv, inv

    tb[own, :] = text_unit()[0].astype(BF)
    pt = rcopy(tb.at[own], tb.at[own], pts, ptr, partner)
    pt.start()

    scale = jnp.exp(jnp.full((1, R), ls_ref[0], F32))
    bias = lb_ref[0]

    def coupling(img, text, positive):
        s = scale * mm(img, text, NT) + bias
        if not positive:
            return (jax.nn.sigmoid(s) * scale).astype(BF)
        rows, cols = s.shape
        diag = lax.broadcasted_iota(jnp.int32, (rows, cols), 0) == lax.broadcasted_iota(
            jnp.int32, (rows, cols), 1
        )
        g = jax.nn.sigmoid(jnp.where(diag, -s, s))
        return (jnp.where(diag, -g, g) * scale).astype(BF)

    def project(rows, slot, n):
        a = xb[rows, :]
        total = jnp.zeros((n, 1), F32)
        for k in range(NCH):
            p = mm(a, wb[:, k * CH : (k + 1) * CH], NN)
            proj[slot, k * CH : (k + 1) * CH] = p
            total = total + jnp.sum(p * p, axis=-1, keepdims=True)
        inv = lax.rsqrt(total + EPS)
        ib[slot, :] = (proj[slot, :] * inv).astype(BF)
        return inv

    def delta_out(tot, slot, inv, col, n):
        unit = proj[slot, :] * inv
        dl = (tot - unit * jnp.sum(unit * tot, axis=-1, keepdims=True)) * inv
        dtf[:, 0:n] = dl.astype(BF).astype(F32).T
        for q in range(2):
            for xx in range(NX):
                for z in range(ZL):
                    o = ((z * NX + xx) * 2 + q) * G
                    pf[z * G : (z + 1) * G, 0:n] = dtf[o : o + G, 0:n]
                dtb[q, xx * ZL * G : (xx + 1) * ZL * G, col] = pf[:, 0:n].astype(BF)

    def dtcopy(col, i):
        return rcopy(
            dtb.at[1 - c, :, col], dtb.at[1 - c, :, col], dts.at[i], dtr.at[i], partner
        )

    lx.wait()
    lw.wait()
    first = pl.ds(0, R)
    inv0 = project(own, first, R)
    cb[...] = coupling(ib[first, :], tb[own, :], True)
    dyo[...] = mm(cb[...], tb[own, :], NN)
    pt.wait()

    @pl.when(c == 1)
    def _():
        c1b[...] = coupling(ib[first, :], tb[0:R, :], False)
        dyo[...] += mm(c1b[...], tb[0:R, :], NN)

    owncol = pl.ds(pl.multiple_of(c * R, R), R)
    delta_out(dyo[...], first, inv0, owncol, R)
    dt0 = dtcopy(owncol, 0)
    dt0.start()

    dyo[...] = mm(cb[...], ib[first, :], TN)

    @pl.when(c == 1)
    def _():
        dys[...] = mm(c1b[...], ib[first, :], TN).astype(BF)

    px.wait()
    dt0.wait()
    for k in range(NCH):
        ks = slice(k * CH, (k + 1) * CH)
        hacc[:, ks] = mm(dtb[c, :, 0 : 2 * R], xb[0 : 2 * R, ks], NN)

    def fwcopy(g, slot):
        rows = pl.ds(pl.multiple_of(2 * R + g * PIECE, PIECE), PIECE)
        return rcopy(xb.at[rows], xb.at[rows], fws.at[slot], fwr.at[slot], partner)

    def colof(g):
        return pl.ds(pl.multiple_of(2 * R + g * PIECE, PIECE), PIECE)

    def piece(g, slot):
        rcopy(
            x_hbm.at[pl.ds(0, PIECE)], xb.at[colof(g)], x2s.at[0], x2r.at[slot], partner
        ).wait_recv()
        fwcopy(g, slot).start()
        at = pl.ds(R + slot * PIECE, PIECE)
        inv = project(colof(g), at, PIECE)
        cp = coupling(ib[at, :], tb[R : 2 * R, :], False)
        c2b[slot * PIECE : (slot + 1) * PIECE, :] = cp
        delta_out(mm(cp, tb[R : 2 * R, :], NN), at, inv, colof(g), PIECE)
        dtcopy(colof(g), 1 + slot).start()

    piece(2 * c, 0)

    @pl.when(c == 0)
    def _():
        piece(1, 1)

    @pl.when(c == 0)
    def _():
        fwcopy(0, 0).wait_send()
        fwcopy(1, 1).wait_send()
        dtcopy(colof(0), 1).wait_send()
        dtcopy(colof(1), 2).wait_send()
        fwcopy(2, 0).wait_recv()
        dtcopy(colof(2), 1).wait_recv()

    @pl.when(c == 1)
    def _():
        fwcopy(2, 0).wait_send()
        dtcopy(colof(2), 1).wait_send()
        fwcopy(0, 0).wait_recv()
        fwcopy(1, 1).wait_recv()
        dtcopy(colof(0), 1).wait_recv()
        dtcopy(colof(1), 2).wait_recv()

    def xcopy(k, d):
        i = k * (NX - 1) + d - 1
        to = (x + d) % NX
        return rcopy(
            xs[k].at[to], xr[k].at[d - 1], xss.at[i], xrs.at[i], dev(to, zl, c, y, zh)
        )

    def zacopy(d):
        to = (zl + d) % ZL
        return rcopy(za.at[to], zar.at[d - 1], zas.at[d - 1], zars.at[d - 1], dev(x, to, c, y, zh))

    def xacopy(d):
        to = (x + d) % NX
        return rcopy(xa.at[to], xar.at[d - 1], xas.at[d - 1], xars.at[d - 1], dev(to, zl, c, y, zh))

    def late(ks):
        hacc[:, ks] += mm(dtb[c, :, 2 * R : 3 * R], xb[2 * R : 3 * R, ks], NN)

    late(slice(FIRST, D))
    for z in range(ZL):
        for xx in range(NX):
            o = (xx * ZL + z) * G
            zaf[z, xx * G : (xx + 1) * G, :] = hacc[o : o + G, FIRST:D]
        za[z] = zaf[z].astype(BF)
    for d in (2, 1, 3):
        zacopy(d).start()
    for k, (o, w) in enumerate(CHUNKS):
        ks = slice(o, o + w)
        late(ks)
        for xx in range(NX):
            xs[k][xx] = hacc[xx * ZL * G : (xx + 1) * ZL * G, ks].astype(BF)
        for d in (2, 1, 3):
            xcopy(k, d).start()

    dyc = rcopy(dys, dyr, dyss, dyrs, partner)

    @pl.when(c == 0)
    def _():
        dys[...] = mm(c2b[...], ib[pl.ds(R, 2 * PIECE), :], TN).astype(BF)

    dyc.start()

    @pl.when(c == 1)
    def _():
        dyo[...] += mm(c2b[0:PIECE, :], ib[pl.ds(R, PIECE), :], TN)

    dyc.wait()
    tu, tinv = text_unit()
    tt = dyo[...] + dyr[...].astype(F32)
    tg_ref[...] = (tt - tu * jnp.sum(tu * tt, axis=-1, keepdims=True)) * tinv

    def zcopy(k, d):
        i = k * (ZL - 1) + d - 1
        to = (zl + d) % ZL
        return rcopy(
            zs[k].at[to], zr[k].at[d - 1], zss.at[i], zrs.at[i], dev(x, to, c, y, zh)
        )

    def ycopy(to):
        slot = (y - to + NY) % NY - 1
        return rcopy(
            ys.at[:, to * 128 : to * 128 + 256],
            yr.at[slot],
            yss.at[to],
            yrs.at[slot],
            dev(x, zl, c, to, zh),
        )

    sc[ZL * G :, :] = jnp.zeros((16, sc.shape[1]), F32)
    rows = pl.ds(pl.multiple_of(x * ZL * G, ZL * G), ZL * G)

    def after_x(k):
        o, w = CHUNKS[k]
        s = hacc[rows, o : o + w]
        for d in range(1, NX):
            xcopy(k, d).wait_recv()
            s = s + xr[k][d - 1].astype(F32)
        sc[0 : ZL * G, 0:w] = s
        for z in range(ZL):
            p = sc[z * G : z * G + 48, 0:w]
            zf[z, :, o : o + w] = p
            zs[k][z] = p.astype(BF)
        for d in range(1, ZL):
            zcopy(k, d).start()

    def after_z(k):
        o, w = CHUNKS[k]
        s = zf[zl, :, o : o + w]
        for d in range(1, ZL):
            zcopy(k, d).wait_recv()
            s = s + zr[k][d - 1].astype(F32)
        yf[:, o : o + w] = s
        ys[:, o : o + w] = s.astype(BF)
        for to in WINDOWS[k]:
            pl.when(y != to)(ycopy(to).start)

    def after_za():
        s = zaf[zl]
        for d in range(1, ZL):
            zacopy(d).wait_recv()
            s = s + zar[d - 1].astype(F32)
        sc[0 : NX * G, 0:WIDE] = s
        for xx in range(NX):
            p = sc[xx * G : xx * G + 48, 0:WIDE]
            xaf[xx] = p
            xa[xx] = p.astype(BF)
        for d in (2, 1, 3):
            xacopy(d).start()

    def after_xa():
        s = xaf[x]
        for d in range(1, NX):
            xacopy(d).wait_recv()
            s = s + xar[d - 1].astype(F32)
        yf[:, FIRST:D] = s
        ys[:, FIRST:D] = s.astype(BF)

    after_za()
    after_x(0)
    after_x(1)
    after_z(0)
    after_xa()
    after_z(1)
    for to in LAST_WINDOWS:
        pl.when(y != to)(ycopy(to).start)
    s = yf[:, pl.ds(pl.multiple_of(y * 128, 128), 256)]
    for d in range(1, NY):
        rcopy(ys.at[:, 0:256], yr.at[d - 1], yss.at[0], yrs.at[d - 1], partner).wait_recv()
        s = s + yr[d - 1].astype(F32)

    for z in range(ZH):
        p = pltpu.roll(s, (256 - (16 * y + 48 * z)) % 256, 1)[:, 0:128]
        hf[z] = p
        hs[z] = p.astype(BF)

    def hcopy(d):
        to = (zh + d) % ZH
        return rcopy(hs.at[to], hr.at[d - 1], hss.at[d - 1], hrs.at[d - 1], dev(x, zl, c, y, to))

    for d in range(1, ZH):
        hcopy(d).start()
    s = hf[zh]
    for d in range(1, ZH):
        hcopy(d).wait_recv()
        s = s + hr[d - 1].astype(F32)
    hg_ref[...] = s[0:G, 0:48]

    @pl.when(c == 0)
    def _():
        for p, core, slot in ((0, 0, 0), (2, 1, 0), (1, 0, 1)):
            x2copy(p, core, slot).wait_send()

    for k in range(len(CHUNKS)):
        for d in range(1, NX):
            xcopy(k, d).wait_send()
        for d in range(1, ZL):
            zcopy(k, d).wait_send()
    for d in range(1, ZL):
        zacopy(d).wait_send()
    for d in range(1, NX):
        xacopy(d).wait_send()
    for to in range(NY):
        pl.when(y != to)(ycopy(to).wait_send)
    for d in range(1, ZH):
        hcopy(d).wait_send()


def shards(image_features, head_weight, text_embeddings, log_scale, logit_bias):
    hbm = pl.BlockSpec(memory_space=pltpu.HBM)
    vmem = pl.BlockSpec(memory_space=pltpu.VMEM)
    smem = pl.BlockSpec(memory_space=pltpu.SMEM)
    dma = pltpu.SemaphoreType.DMA
    V = pltpu.VMEM
    text_grad, head_t = pl.pallas_call(
        kernel,
        out_shape=(pltpu.VMEM((R, D), F32), pltpu.VMEM((G, 48), F32)),
        in_specs=[hbm, hbm, hbm, smem, smem],
        out_specs=(vmem, vmem),
        scratch_shapes=[
            V((3 * R, D), BF),
            V((D, D), BF),
            V((R, D), BF),
            V((2 * R, D), BF),
            V((R + 2 * PIECE, D), F32),
            V((R + 2 * PIECE, D), BF),
            V((R, R), BF),
            V((R, R), BF),
            V((2 * PIECE, R), BF),
            V((R, D), F32),
            V((R, D), BF),
            V((R, D), BF),
            V((D, R), F32),
            V((ZL * G, R), F32),
            V((2, D // 2, D), BF),
            V((D // 2, D), F32),
            *[V((NX, ZL * G, w), BF) for _, w in CHUNKS],
            *[V((NX - 1, ZL * G, w), BF) for _, w in CHUNKS],
            V((ZL * G + 16, max(WIDE, *(w for _, w in CHUNKS))), F32),
            *[V((ZL, 48, w), BF) for _, w in CHUNKS],
            V((ZL, 48, D), F32),
            *[V((ZL - 1, 48, w), BF) for _, w in CHUNKS],
            V((48, D), F32),
            V((48, D), BF),
            V((NY - 1, 48, 256), BF),
            V((ZH, 48, 128), BF),
            V((ZH, 48, 128), F32),
            V((ZH - 1, 48, 128), BF),
            V((ZL, NX * G, WIDE), BF),
            V((ZL, NX * G, WIDE), F32),
            V((ZL - 1, NX * G, WIDE), BF),
            V((NX, 48, WIDE), BF),
            V((NX, 48, WIDE), F32),
            V((NX - 1, 48, WIDE), BF),
            dma((3,)), dma((3,)), dma((2,)), dma((2,)), dma((2,)), dma((3,)), dma((3,)),
            dma, dma, dma, dma, dma, dma,
            *[dma((n,)) for n in (ZL - 1, ZL - 1, NX - 1, NX - 1)],
            dma((NCH * (NX - 1),)), dma((NCH * (NX - 1),)),
            dma((NCH * (ZL - 1),)), dma((NCH * (ZL - 1),)),
            dma((NY,)), dma((NY - 1,)), dma((ZH - 1,)), dma((ZH - 1,)),
        ],
        compiler_params=pltpu.CompilerParams(
            collective_id=0, has_side_effects=True, vmem_limit_bytes=44 * 2**20
        ),
        name="siglip_backward",
    )(
        *(
            pltpu.with_memory_space_constraint(a, pltpu.HBM)
            for a in (image_features, head_weight, text_embeddings)
        ),
        log_scale,
        logit_bias,
    )
    return text_grad, head_t.T


def solution(mesh):
    return jax.shard_map(
        shards,
        mesh=mesh,
        in_specs=(P(("blk", "narrow"), None), P(), P(("blk", "narrow"), None), P(), P()),
        out_specs=(P(("blk", "narrow"), None), P("narrow", "blk")),
        check_vma=False,
    )
```
